512 devices in a mesh: dp: 64 (over z, x, y_hi), rep: 8 (over y_lo, core).
Axes of the slice: x: 4, y: 8 (y_hi: 2, y_lo: 4; y = y_hi * 4 + y_lo), z: 8, core: 2. Of those that a mesh axis runs over, the one named last changes fastest.
Arguments:
- tables: bfloat16 [256, 256, 512], P('dp'), may hold values from -130 to 130
- sample_ids: int32 [512, 256, 4], P('rep', 'dp'), may hold values from 0 to 255
- table_slot: int32 [256], replicated, may hold values from 0 to 255, each once
- norm_gain: float32 [512], replicated, may hold values from 0.5 to 1.5
- qkv_weight: bfloat16 [512, 1152], P('dp'), may hold values from -1.1 to 1.1
- out_weight: bfloat16 [512, 384], P('dp'), may hold values from -0.3125 to 0.3125
- cotangent: bfloat16 [512, 256, 512], P(('rep', 'dp')), may hold values from -24 to 24
Outputs:
- layer_out: bfloat16 [512, 256, 512], P(('rep', 'dp'))
- pooled_grad: bfloat16 [512, 256, 512], P('rep', 'dp')
- grad_qkv: float32 [512, 1152], P('dp')
- grad_out: float32 [512, 384], P('dp')
The draws below stay inside these ranges and needn't reach their ends.
Inputs may be any that keep to these rules, and one draw needn't show every extreme that they name: `table_slot`: each table slot holds the table of exactly one feature.
All inputs are finite; a program needn't handle non-finite values.
Results may differ from the reference program's by a relative error of at most 0.015.
Values may be sent and summed in bfloat16 or wider, within the bound.
A program may use at most 64 MiB of HBM per device.

```python
import math
import jax
import jax.numpy as jnp
from jax import lax

E = 512
H = 6
DH = 64
F = 256
P_SIZE = 4
R = 256
HD = 384
SAMPLES = 512


def draw_tables(key, part):
    keys = jax.random.split(jax.random.fold_in(key, 11), 3)
    row_scale = jnp.exp(jax.random.uniform(keys[1], (F, R, 1), jnp.float32, -1.15, 1.15))
    col_scale = jnp.exp(jax.random.uniform(keys[2], (F, 1, E), jnp.float32, -1.15, 1.15))
    base = jnp.clip(jax.random.normal(keys[0], (F, R, E), jnp.float32), -4.0, 4.0)
    return (row_scale * col_scale * base).astype(jnp.bfloat16)


def draw_qkv_weight(key, part):
    keys = jax.random.split(jax.random.fold_in(key, 23), 1)
    base = jnp.clip(jax.random.normal(keys[0], (E, 3 * H * DH), jnp.float32), -4.0, 4.0) / math.sqrt(E)
    return jnp.clip(base, -1.1, 1.1).astype(jnp.bfloat16)


def plant(result, own_key, low, top_value):
    shape = result.shape
    place = [jax.random.randint(jax.random.fold_in(own_key, axis), (), 0, shape[axis]) for axis in range(len(shape))]
    result = result.at[tuple(place)].set(low)
    longest = shape.index(max(shape))
    place[longest] = (place[longest] + 1) % shape[longest]
    return result.at[tuple(place)].set(top_value)


def spiked(values, key, source, target, shards_of, factor):
    def block_of(position):
        return (jnp.arange(values.shape[position]) // (values.shape[position] // shards_of)).reshape((-1,) + (1,) * (values.ndim - 1 - position))

    one_side = jax.random.permutation(key, shards_of)[block_of(target)]
    second = (block_of(target) + shards_of // 2) % shards_of
    return jnp.where((block_of(source) == one_side) | (block_of(source) == second), factor * values, values)


def levels(rng, shape, cuts, smallest, high):
    def one(dim, parts):
        steps = jax.random.uniform(jax.random.fold_in(jax.random.fold_in(rng, 6), dim), (parts,), jnp.float32, smallest / len(cuts), high / len(cuts))
        return jnp.repeat(jnp.exp(steps), shape[dim] // parts).reshape((-1,) + (1,) * (len(shape) - dim - 1))

    loudness = one(*cuts[0])
    for cut in cuts[1:]:
        loudness = loudness * one(*cut)
    return loudness


def centred(stream_key, shape, scale, reach, cuts=(), kind=jnp.bfloat16):
    gain = levels(stream_key, shape, cuts, -0.22, 0.18) if cuts else 1.0
    values = jax.random.normal(stream_key, shape, jnp.float32) * scale * gain
    return jnp.minimum(jnp.maximum(values, -reach), reach).astype(kind)


def gaussian_with(rng, shape, scale, limit, cuts, heavy, kind=jnp.bfloat16):
    result = scale * jax.random.normal(rng, shape, jnp.float32)
    if cuts:
        result = result * levels(rng, shape, cuts, -0.22, 0.18)
    return jnp.clip(spiked(result, jax.random.fold_in(rng, 3), *heavy), -limit, limit).astype(kind)


def setup_inputs(seed: int = 0) -> dict:
    key_of = jax.random.split(jax.random.key(seed), 8)
    tables = draw_tables(jax.random.fold_in(key_of[7], 71), 0)
    sample_ids = plant(jax.random.randint(key_of[1], (SAMPLES, F, P_SIZE), 0, R), jax.random.fold_in(key_of[1], 1), 0, R - 1).astype(jnp.int32)
    table_slot = jax.random.permutation(key_of[2], F).astype(jnp.int32)
    norm_gain = jnp.clip(1.0 + 0.1 * jax.random.normal(key_of[3], (E,), jnp.float32), 0.5, 1.5)
    qkv_weight = draw_qkv_weight(jax.random.fold_in(key_of[7], 71), 0)
    out_weight = centred(key_of[5], (E, HD), HD ** -0.5, 0.3125, ((0, 64),))
    cotangent = gaussian_with(key_of[6], (SAMPLES, F, E), 1.0, 24.0, ((0, 512),), (0, 2, 512, 6.0))
    return {"tables": tables, "sample_ids": sample_ids, "table_slot": table_slot, "norm_gain": norm_gain, "qkv_weight": qkv_weight, "out_weight": out_weight, "cotangent": cotangent}


norm_eps = 1e-06
sample_block = 8

def attend(projected, sample_count):
    projected_split = lax.optimization_barrier(projected).reshape(sample_count, F, 3, H, DH).astype(jnp.float32)
    query_part = projected_split[:, :, 0]
    key_part = projected_split[:, :, 1]
    value_part = projected_split[:, :, 2]
    scores = jnp.einsum('sqhd,skhd->shqk', query_part, key_part) * DH ** (-0.5)
    shifted = scores - lax.optimization_barrier(jnp.max(scores, axis=-1, keepdims=True))
    raised = jnp.exp(shifted)
    soft = (raised / lax.optimization_barrier(jnp.sum(raised, axis=-1, keepdims=True))).astype(jnp.bfloat16)
    soft = lax.optimization_barrier(soft)
    context = jnp.einsum('shqk,skhd->sqhd', soft.astype(jnp.float32), value_part).astype(jnp.bfloat16)
    return (context.reshape(sample_count * F, H * DH), soft, query_part, key_part, value_part)

def attend_back(grad_context, soft, query_part, key_part, value_part, sample_count):
    grad_ctx = lax.optimization_barrier(grad_context).reshape(sample_count, F, H, DH).astype(jnp.float32)
    soft_float = soft.astype(jnp.float32)
    grad_soft = jnp.einsum('sqhd,skhd->shqk', grad_ctx, value_part)
    inner = lax.optimization_barrier(jnp.sum(soft_float * grad_soft, axis=-1, keepdims=True))
    grad_scores = (soft_float * (grad_soft - inner) * DH ** (-0.5)).astype(jnp.bfloat16)
    grad_scores = lax.optimization_barrier(grad_scores).astype(jnp.float32)
    grad_query = jnp.einsum('shqk,skhd->sqhd', grad_scores, key_part).astype(jnp.bfloat16)
    grad_key = jnp.einsum('shqk,sqhd->skhd', grad_scores, query_part).astype(jnp.bfloat16)
    grad_value = jnp.einsum('shqk,sqhd->skhd', soft_float, grad_ctx).astype(jnp.bfloat16)
    stacked = jnp.stack([grad_query, grad_key, grad_value], axis=2)
    return stacked.reshape(sample_count * F, 3 * H * DH)

def layer_pass(tokens, cotangent, norm_gain, qkv_weight, out_weight):
    sample_count = tokens.shape[0]
    row_count = sample_count * F
    token_rows = tokens.reshape(row_count, E)
    cot_rows = cotangent.reshape(row_count, E)
    as_float = token_rows.astype(jnp.float32)
    inverse_rms = lax.rsqrt(lax.optimization_barrier(jnp.mean(as_float * as_float, axis=-1, keepdims=True)) + norm_eps)
    normed = as_float * inverse_rms
    gain_float = norm_gain.astype(jnp.float32)
    hidden = (normed * gain_float).astype(jnp.bfloat16)
    projected = jnp.dot(hidden, qkv_weight, preferred_element_type=jnp.float32).astype(jnp.bfloat16)
    context, soft, query_part, key_part, value_part = attend(projected, sample_count)
    mixed_rows = as_float + jnp.dot(context, out_weight.T, preferred_element_type=jnp.float32)
    layer_out = mixed_rows.astype(jnp.bfloat16)
    grad_out = jnp.dot(cot_rows.T, context, preferred_element_type=jnp.float32)
    grad_context = jnp.dot(cot_rows, out_weight, preferred_element_type=jnp.float32).astype(jnp.bfloat16)
    grad_projected = attend_back(grad_context, soft, query_part, key_part, value_part, sample_count)
    grad_qkv = jnp.dot(hidden.T, grad_projected, preferred_element_type=jnp.float32)
    grad_hidden = jnp.dot(grad_projected, qkv_weight.T, preferred_element_type=jnp.float32)
    scaled = grad_hidden * gain_float
    grad_norm = inverse_rms * (scaled - normed * lax.optimization_barrier(jnp.mean(scaled * normed, axis=-1, keepdims=True)))
    grad_tokens = (cot_rows.astype(jnp.float32) + grad_norm).astype(jnp.bfloat16)
    return (layer_out.reshape(sample_count, F, E), grad_tokens.reshape(sample_count, F, E), grad_qkv, grad_out)

def reference(tables, sample_ids, table_slot, norm_gain, qkv_weight, out_weight, cotangent):
    inverse_slot = jnp.zeros((F,), jnp.int32).at[table_slot].set(jnp.arange(F, dtype=jnp.int32))
    block_count = SAMPLES // sample_block
    id_blocks = sample_ids.reshape(block_count, sample_block, F, P_SIZE)
    cot_blocks = cotangent.reshape(block_count, sample_block, F, E)
    slot_index = jnp.arange(F, dtype=jnp.int32)[None, :, None]

    def scan_step(carried, block_pair):
        id_part, cot_part = block_pair
        gathered = tables[slot_index, id_part].astype(jnp.float32)
        pooled = (lax.optimization_barrier(jnp.sum(gathered, axis=2)) * (1.0 / math.sqrt(P_SIZE))).astype(jnp.bfloat16)
        tokens = jnp.take(pooled, table_slot, axis=1)
        layer_out, grad_tokens, grad_qkv, grad_out = layer_pass(tokens, cot_part, norm_gain, qkv_weight, out_weight)
        grad_pooled = jnp.take(grad_tokens, inverse_slot, axis=1)
        return ((carried[0] + grad_qkv, carried[1] + grad_out), (layer_out, grad_pooled))
    initial = (jnp.zeros((E, 3 * H * DH), jnp.float32), jnp.zeros((E, H * DH), jnp.float32))
    sums, outputs = lax.scan(scan_step, initial, (id_blocks, cot_blocks))
    scale_back = 1.0 / SAMPLES
    layer_out = outputs[0].reshape(SAMPLES, F, E)
    pooled_grad = outputs[1].reshape(SAMPLES, F, E)
    return (layer_out, pooled_grad, sums[0] * scale_back, sums[1] * scale_back)
```

```python
import jax
import jax.numpy as jnp
from jax import lax
from jax.experimental import pallas as pl
from jax.experimental.pallas import tpu as pltpu
from jax.sharding import PartitionSpec as P

E = 512
H = 6
DH = 64
F = 256
P_SIZE = 4
HD = H * DH
SAMPLES = 512
EPS = 1e-06

NX = 4
NZ = 8
NY = 8
NDP = 64

BF = jnp.bfloat16
F32 = jnp.float32
MESH = pl.DeviceIdType.MESH


def dot(a, b, ca, cb):
    return lax.dot_general(a, b, (((ca,), (cb,)), ((), ())), preferred_element_type=F32)


def fused(
    tables,
    ids,
    slot,
    gain,
    qkv,
    outw,
    cot,
    layer_out,
    pooled_grad,
    grad_qkv,
    grad_out,
    rows_f,
    tok_send,
    tok_recv,
    gt_send,
    gt_recv,
    w_send,
    w_all,
    wq,
    wo,
    g_all,
    sib_recv,
    x_recv,
    s2,
    z_recv,
    s3,
    y_recv,
    fin,
    send_sem,
    recv_sem,
    wx_sem,
    gs_sem,
):
    dp = lax.axis_index("dp")
    rep = lax.axis_index("rep")
    z = dp // 8
    x = lax.rem(dp // 2, 4)
    yh = lax.rem(dp, 2)
    yl = rep // 2
    core = lax.rem(rep, 2)
    other = 1 - core
    y = yh * 4 + yl
    sib = (dp, yl * 2 + other)

    def dp_of(zz, xx, hh):
        return zz * 8 + xx * 2 + hh

    def y_peer(k):
        yy = lax.rem(y + k, NY)
        return yy // 4, (dp_of(z, x, yy // 4), lax.rem(yy, 4) * 2 + core)

    def send(src, dst, ssem, rsem, who):
        pltpu.make_async_remote_copy(
            src_ref=src,
            dst_ref=dst,
            send_sem=ssem,
            recv_sem=rsem,
            device_id=who,
            device_id_type=MESH,
        ).start()

    def drain(ref, sem):
        pltpu.make_async_copy(ref, ref, sem).wait()

    barrier = pltpu.get_barrier_semaphore()

    def greet(k, carry):
        pl.semaphore_signal(
            barrier, inc=1, device_id=(lax.rem(dp + k, NDP), rep), device_id_type=MESH
        )
        return carry

    lax.fori_loop(1, NDP, greet, 0)
    pl.semaphore_signal(barrier, inc=1, device_id=sib, device_id_type=MESH)
    for k in range(1, NY):
        pl.semaphore_signal(barrier, inc=1, device_id=y_peer(k)[1], device_id_type=MESH)

    wide = jnp.concatenate([qkv[...].astype(F32), outw[...].astype(F32)], axis=1)
    for k in range(6):
        pair = jnp.concatenate(
            [wide[:, 256 * k : 256 * k + 128], wide[:, 256 * k + 128 : 256 * k + 256]], axis=0
        ).astype(BF)
        w_send[k // 3, 16 * (k % 3) : 16 * (k % 3) + 16, :] = pair
    w_all[core, x, z * 2 + yh] = w_send[core]

    row_iota = lax.broadcasted_iota(jnp.int32, (F, NDP), 0)
    for j in range(4):
        counts = jnp.zeros((F, NDP), F32)
        for p in range(P_SIZE):
            counts = counts + jnp.where(row_iota == ids[4 * j + p : 4 * j + p + 1, :], 1.0, 0.0)
        pooled = dot(counts.astype(BF), tables[j], 0, 0) * 0.5
        for cb in range(4):
            rows_f[pl.ds(4 * j + cb, NDP, stride=16), :] = pooled[:, 128 * cb : 128 * cb + 128]
    tok_send[...] = rows_f[...].astype(BF).reshape(NDP, 16, 128)
    tok_recv[dp] = tok_send[dp]

    pl.semaphore_wait(barrier, NDP - 1 + 1 + NY - 1)

    for k in range(1, 16):
        q = lax.rem(z * 2 + yh + k, 16)
        send(
            w_send.at[core],
            w_all.at[core, x, z * 2 + yh],
            send_sem.at[0],
            recv_sem.at[0],
            (dp_of(q // 2, x, lax.rem(q, 2)), rep),
        )

    def send_tok(k, carry):
        p = lax.rem(dp + k, NDP)
        send(tok_send.at[p], tok_recv.at[dp], send_sem.at[1], recv_sem.at[1], (p, rep))
        return carry

    lax.fori_loop(1, NDP, send_tok, 0)

    drain(w_all.at[core, x, pl.ds(0, 15)], recv_sem.at[0])
    for k in (1, 3, 2):
        send(
            w_all.at[core, x],
            w_all.at[core, x],
            send_sem.at[2],
            wx_sem.at[k - 1],
            (dp_of(z, lax.rem(x + k, NX), yh), rep),
        )
    send(w_all.at[core, x], w_all.at[core, x], send_sem.at[3], recv_sem.at[2], sib)
    for k in (1, 3, 2):
        xx = lax.rem(x + NX - k, NX)
        drain(w_all.at[core, xx], wx_sem.at[k - 1])
        send(w_all.at[core, xx], w_all.at[core, xx], send_sem.at[3], recv_sem.at[2], sib)

    drain(tok_recv.at[pl.ds(0, NDP - 1)], recv_sem.at[1])
    rows_f[...] = tok_recv[...].reshape(NDP * 16, 128).astype(F32)
    by_slot = jnp.concatenate(
        [rows_f[pl.ds(cb, F, stride=4), :] for cb in range(4)], axis=1
    ).astype(BF)
    slot_iota = lax.broadcasted_iota(jnp.int32, (F, F), 0)
    place = jnp.where(slot_iota == slot[...], 1.0, 0.0).astype(BF)
    tokens = dot(place, by_slot, 0, 0)
    inv = lax.rsqrt(jnp.mean(tokens * tokens, axis=-1, keepdims=True) + EPS)
    normed = tokens * inv
    gains = gain[...]
    hidden = (normed * gains).astype(BF)

    drain(w_all.at[other], recv_sem.at[2])
    for k in range(6):
        c, part = k // 3, k % 3
        for xx in range(NX):
            both = w_all[c, xx, :, 16 * part : 16 * part + 16, :].astype(F32)
            both = both.reshape(NZ, 2, 2, 8, 128)
            for half in range(2):
                block = both[:, :, half].reshape(NZ, 16, 128).astype(BF)
                cb = 2 * k + half
                for zz in range(NZ):
                    r0 = 64 * zz + 16 * xx
                    if cb < 9:
                        wq[r0 : r0 + 16, 128 * cb : 128 * cb + 128] = block[zz]
                    else:
                        wo[r0 : r0 + 16, 128 * (cb - 9) : 128 * (cb - 9) + 128] = block[zz]

    grad_context = dot(cot[...], wo[...], 1, 0).astype(BF)
    projected = dot(hidden, wq[...], 1, 0).astype(BF)
    low = lax.broadcasted_iota(jnp.int32, (F, 128), 1) < DH
    zero = jnp.zeros((F, 128), BF)
    contexts, gq, gk, gv = [], [], [], []
    for i in range(H // 2):
        q2 = projected[:, 128 * i : 128 * i + 128]
        k2 = projected[:, HD + 128 * i : HD + 128 * i + 128]
        v2 = projected[:, 2 * HD + 128 * i : 2 * HD + 128 * i + 128]
        c2 = grad_context[:, 128 * i : 128 * i + 128]
        parts = []
        for half in range(2):
            mine = low if half == 0 else jnp.logical_not(low)
            scores = dot(jnp.where(mine, q2, zero), k2, 1, 1) * DH ** (-0.5)
            raised = jnp.exp(scores - jnp.max(scores, axis=-1, keepdims=True))
            soft = (raised / jnp.sum(raised, axis=-1, keepdims=True)).astype(BF)
            context = dot(soft, v2, 1, 0)
            grad_soft = dot(jnp.where(mine, c2, zero), v2, 1, 1)
            soft_f = soft.astype(F32)
            inner = jnp.sum(soft_f * grad_soft, axis=-1, keepdims=True)
            gs = (soft_f * (grad_soft - inner) * DH ** (-0.5)).astype(BF)
            parts.append((context, dot(gs, k2, 1, 0), dot(gs, q2, 0, 0), dot(soft, c2, 0, 0)))
        for out, a, b in zip((contexts, gq, gk, gv), parts[0], parts[1]):
            out.append(jnp.where(low, a, b).astype(BF))
    context = jnp.concatenate(contexts, axis=1)
    grad_projected = jnp.concatenate(gq + gk + gv, axis=1)

    for k in range(6):
        c, part = k // 3, k % 3
        blocks = []
        for cb in (2 * k, 2 * k + 1):
            if cb < 9:
                g = dot(hidden, grad_projected[:, 128 * cb : 128 * cb + 128], 0, 0)
            else:
                g = dot(cot[...], context[:, 128 * (cb - 9) : 128 * (cb - 9) + 128], 0, 0)
            blocks.append(g.reshape(NZ, NX, 2, 8, 128))
        both = jnp.concatenate(blocks, axis=3).astype(BF)
        for xx in range(NX):
            g_all[c, xx, :, 16 * part : 16 * part + 16, :] = both[:, xx].reshape(16, 16, 128)

    for k in range(NX):
        xx = lax.rem(x + 1 + k, NX)
        send(g_all.at[other, xx], sib_recv.at[xx], send_sem.at[4], gs_sem.at[k], sib)

    layer_out[...] = (tokens + dot(context, wo[...], 1, 1)).astype(BF)
    scaled = dot(grad_projected, wq[...], 1, 1) * gains
    grad_norm = inv * (scaled - normed * jnp.mean(scaled * normed, axis=-1, keepdims=True))
    grad_tokens = (cot[...].astype(F32) + grad_norm).astype(BF)
    grad_slots = dot(place, grad_tokens, 1, 0)
    for cb in range(4):
        rows_f[pl.ds(cb, F, stride=4), :] = grad_slots[:, 128 * cb : 128 * cb + 128]
    gt_send[...] = rows_f[...].astype(BF).reshape(NDP, 16, 128)

    for k in range(NX):
        xx = lax.rem(x + 1 + k, NX)
        drain(sib_recv.at[xx], gs_sem.at[k])
        total = g_all[core, xx].astype(F32) + sib_recv[xx].astype(F32)
        if k < NX - 1:
            g_all[core, xx] = total.astype(BF)
            send(
                g_all.at[core, xx],
                x_recv.at[k],
                send_sem.at[5],
                recv_sem.at[3],
                (dp_of(z, xx, yh), rep),
            )

    def send_grad(k, carry):
        p = lax.rem(dp + k, NDP)
        send(gt_send.at[p], gt_recv.at[dp], send_sem.at[6], recv_sem.at[4], (p, rep))
        return carry

    lax.fori_loop(1, NDP, send_grad, 0)
    gt_recv[dp] = gt_send[dp]

    drain(x_recv, recv_sem.at[3])
    for k in range(NX - 1):
        total = total + x_recv[k].astype(F32)
    s2[...] = total.astype(BF).reshape(NZ, 2, 48, 128)

    for k in range(1, NZ):
        zz = lax.rem(z + k, NZ)
        send(
            s2.at[zz], z_recv.at[k - 1], send_sem.at[7], recv_sem.at[5], (dp_of(zz, x, yh), rep)
        )
    total = s2[z].astype(F32)
    drain(z_recv, recv_sem.at[5])
    for k in range(NZ - 1):
        total = total + z_recv[k].astype(F32)
    s3[...] = total.astype(BF)

    for k in range(1, NY):
        hh, who = y_peer(k)
        send(s3.at[hh], y_recv.at[k - 1], send_sem.at[8], recv_sem.at[6], who)
    total = s3[yh].astype(F32)
    drain(y_recv, recv_sem.at[6])
    for k in range(NY - 1):
        total = total + y_recv[k].astype(F32)
    fin[core] = total * (1.0 / SAMPLES)
    send(fin.at[core], fin.at[core], send_sem.at[9], recv_sem.at[7], sib)

    drain(gt_recv.at[pl.ds(0, NDP - 1)], recv_sem.at[4])
    pooled_grad[...] = gt_recv[...]
    drain(fin.at[other], recv_sem.at[7])
    for cb in range(12):
        piece = fin[cb // 6, 8 * (cb % 6) : 8 * (cb % 6) + 8, :]
        if cb < 9:
            grad_qkv[:, 128 * cb : 128 * cb + 128] = piece
        else:
            grad_out[:, 128 * (cb - 9) : 128 * (cb - 9) + 128] = piece

    drain(w_all.at[core, x, pl.ds(0, 15)], send_sem.at[0])
    drain(tok_send.at[pl.ds(0, NDP - 1)], send_sem.at[1])
    drain(w_all.at[core, pl.ds(0, 3)], send_sem.at[2])
    drain(w_all.at[core], send_sem.at[3])
    drain(sib_recv, send_sem.at[4])
    drain(x_recv, send_sem.at[5])
    drain(gt_send.at[pl.ds(0, NDP - 1)], send_sem.at[6])
    drain(z_recv, send_sem.at[7])
    drain(y_recv, send_sem.at[8])
    drain(fin.at[core], send_sem.at[9])


def on_device(tables, sample_ids, table_slot, norm_gain, qkv_weight, out_weight, cotangent):
    vmem = pl.BlockSpec(memory_space=pltpu.VMEM)
    layer_out, pooled_grad, grad_qkv, grad_out = pl.pallas_call(
        fused,
        out_shape=(
            jax.ShapeDtypeStruct((F, E), BF),
            jax.ShapeDtypeStruct((NDP, 16, 128), BF),
            jax.ShapeDtypeStruct((8, 3 * HD), F32),
            jax.ShapeDtypeStruct((8, HD), F32),
        ),
        in_specs=[vmem] * 7,
        out_specs=(vmem,) * 4,
        scratch_shapes=[
            pltpu.VMEM((NDP * 16, 128), F32),
            pltpu.VMEM((NDP, 16, 128), BF),
            pltpu.VMEM((NDP, 16, 128), BF),
            pltpu.VMEM((NDP, 16, 128), BF),
            pltpu.VMEM((NDP, 16, 128), BF),
            pltpu.VMEM((2, 48, 128), BF),
            pltpu.VMEM((2, NX, 16, 48, 128), BF),
            pltpu.VMEM((E, 3 * HD), BF),
            pltpu.VMEM((E, HD), BF),
            pltpu.VMEM((2, NX, 16, 48, 128), BF),
            pltpu.VMEM((NX, 16, 48, 128), BF),
            pltpu.VMEM((NX - 1, 16, 48, 128), BF),
            pltpu.VMEM((NZ, 2, 48, 128), BF),
            pltpu.VMEM((NZ - 1, 2, 48, 128), BF),
            pltpu.VMEM((2, 48, 128), BF),
            pltpu.VMEM((NY - 1, 48, 128), BF),
            pltpu.VMEM((2, 48, 128), F32),
            pltpu.SemaphoreType.DMA((10,)),
            pltpu.SemaphoreType.DMA((8,)),
            pltpu.SemaphoreType.DMA((3,)),
            pltpu.SemaphoreType.DMA((4,)),
        ],
        compiler_params=pltpu.CompilerParams(
            collective_id=0, has_side_effects=True, vmem_limit_bytes=48 * 1024 * 1024
        ),
        cost_estimate=pl.CostEstimate(
            flops=2_000_000_000, bytes_accessed=4_000_000, transcendentals=400_000
        ),
    )(
        tables,
        jnp.transpose(sample_ids, (1, 2, 0)).reshape(16, NDP),
        table_slot.reshape(1, F),
        norm_gain.reshape(1, E),
        qkv_weight,
        out_weight,
        cotangent.reshape(F, E),
    )
    return (
        layer_out.reshape(1, F, E),
        pooled_grad.reshape(NDP, 4, E),
        grad_qkv,
        grad_out,
    )


def solution(mesh):
    return jax.shard_map(
        on_device,
        mesh=mesh,
        in_specs=(
            P("dp", None, None),
            P("rep", "dp", None),
            P(),
            P(),
            P("dp", None),
            P("dp", None),
            P(("rep", "dp"), None, None),
        ),
        out_specs=(
            P(("rep", "dp"), None, None),
            P("rep", "dp", None),
            P("dp", None),
            P("dp", None),
        ),
        check_vma=False,
    )
```

```python
import jax
import jax.numpy as jnp
from jax import lax
from jax.experimental import pallas as pl
from jax.experimental.pallas import tpu as pltpu
from jax.sharding import PartitionSpec as P

E = 512
H = 6
DH = 64
F = 256
P_SIZE = 4
HD = H * DH
SAMPLES = 512
EPS = 1e-06

NX = 4
NZ = 8
NY = 8
NDP = 64

BF = jnp.bfloat16
F32 = jnp.float32
MESH = pl.DeviceIdType.MESH


def dot(a, b, ca, cb):
    return lax.dot_general(a, b, (((ca,), (cb,)), ((), ())), preferred_element_type=F32)


def fused(
    tables_h,
    ids_h,
    slot_h,
    gain_h,
    qkv,
    outw,
    cot_h,
    layer_out_h,
    pooled_grad_h,
    grad_qkv_h,
    grad_out_h,
    tables,
    ids,
    slot,
    gain,
    cot,
    rows_f,
    tok_send,
    tok_recv,
    gt_send,
    gt_recv,
    w_send,
    w_all,
    wq,
    wo,
    g_all,
    sib_recv,
    x_recv,
    s2,
    z_recv,
    s3,
    y_recv,
    fin,
    send_sem,
    recv_sem,
    w_sem,
    wx_sem,
    ws_sem,
    sib_sem,
    x_sem,
    z_sem,
    y_sem,
    fin_sem,
    in_sem,
    layer_out,
    grad_qkv,
    grad_out,
    out_sem,
):
    dp = lax.axis_index("dp")
    rep = lax.axis_index("rep")
    z = dp // 8
    x = lax.rem(dp // 2, 4)
    yh = lax.rem(dp, 2)
    yl = rep // 2
    core = lax.rem(rep, 2)
    other = 1 - core
    y = yh * 4 + yl
    sib = (dp, yl * 2 + other)

    def dp_of(zz, xx, hh):
        return zz * 8 + xx * 2 + hh

    def y_peer(k):
        yy = lax.rem(y + k, NY)
        return yy // 4, (dp_of(z, x, yy // 4), lax.rem(yy, 4) * 2 + core)

    def send(src, dst, ssem, rsem, who):
        pltpu.make_async_remote_copy(
            src_ref=src,
            dst_ref=dst,
            send_sem=ssem,
            recv_sem=rsem,
            device_id=who,
            device_id_type=MESH,
        ).start()

    def drain(ref, sem):
        pltpu.make_async_copy(ref, ref, sem).wait()

    barrier = pltpu.get_barrier_semaphore()

    def greet(k, carry):
        pl.semaphore_signal(
            barrier, inc=1, device_id=(lax.rem(dp + k, NDP), rep), device_id_type=MESH
        )
        return carry

    lax.fori_loop(1, NDP, greet, 0)
    pl.semaphore_signal(barrier, inc=1, device_id=sib, device_id_type=MESH)
    for k in range(1, NY):
        pl.semaphore_signal(barrier, inc=1, device_id=y_peer(k)[1], device_id_type=MESH)

    def load(i, src, dst):
        pltpu.make_async_copy(src, dst, in_sem.at[i]).start()

    def loaded(i, src, dst):
        pltpu.make_async_copy(src, dst, in_sem.at[i]).wait()

    inputs = (
        (ids_h, ids),
        (tables_h, tables),
        (slot_h, slot),
        (gain_h, gain),
        (cot_h, cot),
    )
    for i, (src, dst) in enumerate(inputs):
        load(i, src, dst)

    wide = jnp.concatenate([qkv[...].astype(F32), outw[...].astype(F32)], axis=1)
    for k in range(6):
        pair = jnp.concatenate(
            [wide[:, 256 * k : 256 * k + 128], wide[:, 256 * k + 128 : 256 * k + 256]], axis=0
        ).astype(BF)
        w_send[k // 3, k % 3] = pair
    for part in range(3):
        w_all[core, part, x, z * 2 + yh] = w_send[core, part]

    pl.semaphore_wait(barrier, NDP - 1 + 1 + NY - 1)

    for part in range(3):
        for k in range(1, 16):
            q = lax.rem(z * 2 + yh + k, 16)
            send(
                w_send.at[core, part],
                w_all.at[core, part, x, z * 2 + yh],
                send_sem.at[0],
                w_sem.at[part],
                (dp_of(q // 2, x, lax.rem(q, 2)), rep),
            )

    loaded(0, *inputs[0])
    loaded(1, *inputs[1])
    row_iota = lax.broadcasted_iota(jnp.int32, (F, NDP), 0)
    for j in range(4):
        counts = jnp.zeros((F, NDP), F32)
        for p in range(P_SIZE):
            counts = counts + jnp.where(row_iota == ids[4 * j + p : 4 * j + p + 1, :], 1.0, 0.0)
        pooled = dot(counts.astype(BF), tables[j], 0, 0) * 0.5
        for cb in range(4):
            rows_f[pl.ds(4 * j + cb, NDP, stride=16), :] = pooled[:, 128 * cb : 128 * cb + 128]
    tok_send[...] = rows_f[...].astype(BF).reshape(NDP, 16, 128)
    tok_recv[dp] = tok_send[dp]

    def send_tok(k, carry):
        p = lax.rem(dp + k, NDP)
        send(tok_send.at[p], tok_recv.at[dp], send_sem.at[1], recv_sem.at[1], (p, rep))
        return carry

    lax.fori_loop(1, NDP, send_tok, 0)

    def to_sibling(part, xx):
        block = w_all.at[core, part, xx]
        send(block, block, send_sem.at[3], ws_sem.at[part], sib)

    def forward(part):
        for k in (1, 3, 2):
            xx = lax.rem(x + NX - k, NX)
            drain(w_all.at[core, part, xx], wx_sem.at[part, k - 1])
            to_sibling(part, xx)

    for part in range(3):
        block = w_all.at[core, part, x]
        drain(w_all.at[core, part, x, pl.ds(0, 15)], w_sem.at[part])
        for k in (1, 3, 2):
            send(
                block,
                block,
                send_sem.at[2],
                wx_sem.at[part, k - 1],
                (dp_of(z, lax.rem(x + k, NX), yh), rep),
            )
        to_sibling(part, x)
    forward(0)
    forward(1)

    drain(tok_recv.at[pl.ds(0, NDP - 1)], recv_sem.at[1])
    rows_f[...] = tok_recv[...].reshape(NDP * 16, 128).astype(F32)
    by_slot = jnp.concatenate(
        [rows_f[pl.ds(cb, F, stride=4), :] for cb in range(4)], axis=1
    ).astype(BF)
    loaded(2, *inputs[2])
    loaded(3, *inputs[3])
    slot_iota = lax.broadcasted_iota(jnp.int32, (F, F), 0)
    place = jnp.where(slot_iota == slot[...], 1.0, 0.0).astype(BF)
    tokens = dot(place, by_slot, 0, 0)
    inv = lax.rsqrt(jnp.mean(tokens * tokens, axis=-1, keepdims=True) + EPS)
    normed = tokens * inv
    gains = gain[...]
    hidden = (normed * gains).astype(BF)

    forward(2)
    for part in range(3):
        drain(w_all.at[other, part], ws_sem.at[part])
        for k in (part, part + 3):
            for xx in range(NX):
                both = w_all[k // 3, part, xx].astype(F32).reshape(NZ, 2, 2, 8, 128)
                for half in range(2):
                    block = both[:, :, half].reshape(NZ, 16, 128).astype(BF)
                    cb = 2 * k + half
                    for zz in range(NZ):
                        r0 = 64 * zz + 16 * xx
                        if cb < 9:
                            wq[r0 : r0 + 16, 128 * cb : 128 * cb + 128] = block[zz]
                        else:
                            wo[r0 : r0 + 16, 128 * (cb - 9) : 128 * (cb - 9) + 128] = block[zz]

    loaded(4, *inputs[4])
    grad_context = dot(cot[...], wo[...], 1, 0).astype(BF)
    projected = dot(hidden, wq[...], 1, 0).astype(BF)
    low = lax.broadcasted_iota(jnp.int32, (F, 128), 1) < DH
    zero = jnp.zeros((F, 128), BF)
    contexts, gq, gk, gv = [], [], [], []
    for i in range(H // 2):
        q2 = projected[:, 128 * i : 128 * i + 128]
        k2 = projected[:, HD + 128 * i : HD + 128 * i + 128]
        v2 = projected[:, 2 * HD + 128 * i : 2 * HD + 128 * i + 128]
        c2 = grad_context[:, 128 * i : 128 * i + 128]
        parts = []
        for half in range(2):
            mine = low if half == 0 else jnp.logical_not(low)
            scores = dot(jnp.where(mine, q2, zero), k2, 1, 1) * DH ** (-0.5)
            raised = jnp.exp(scores - jnp.max(scores, axis=-1, keepdims=True))
            soft = (raised / jnp.sum(raised, axis=-1, keepdims=True)).astype(BF)
            context = dot(soft, v2, 1, 0)
            grad_soft = dot(jnp.where(mine, c2, zero), v2, 1, 1)
            soft_f = soft.astype(F32)
            inner = jnp.sum(soft_f * grad_soft, axis=-1, keepdims=True)
            gs = (soft_f * (grad_soft - inner) * DH ** (-0.5)).astype(BF)
            parts.append((context, dot(gs, k2, 1, 0), dot(gs, q2, 0, 0), dot(soft, c2, 0, 0)))
        for out, a, b in zip((contexts, gq, gk, gv), parts[0], parts[1]):
            out.append(jnp.where(low, a, b).astype(BF))
    context = jnp.concatenate(contexts, axis=1)
    grad_projected = jnp.concatenate(gq + gk + gv, axis=1)

    for part in range(3):
        for c in range(2):
            k = 3 * c + part
            blocks = []
            for cb in (2 * k, 2 * k + 1):
                if cb < 9:
                    g = dot(hidden, grad_projected[:, 128 * cb : 128 * cb + 128], 0, 0)
                else:
                    g = dot(cot[...], context[:, 128 * (cb - 9) : 128 * (cb - 9) + 128], 0, 0)
                blocks.append(g.reshape(NZ, NX, 2, 8, 128))
            both = jnp.concatenate(blocks, axis=3).astype(BF)
            for xx in range(NX):
                g_all[c, part, xx] = both[:, xx].reshape(16, 16, 128)
        send(g_all.at[other, part], sib_recv.at[part], send_sem.at[4], sib_sem.at[part], sib)

    scaled = dot(grad_projected, wq[...], 1, 1) * gains
    grad_norm = inv * (scaled - normed * jnp.mean(scaled * normed, axis=-1, keepdims=True))
    grad_tokens = (cot[...].astype(F32) + grad_norm).astype(BF)
    turned = lax.rem(slot_iota, NDP) * 4 + slot_iota // NDP
    place_back = jnp.where(turned == slot[...], 1.0, 0.0).astype(BF)
    grad_slots = dot(place_back, grad_tokens, 1, 0)
    for cb in range(4):
        for j in range(4):
            rows_f[pl.ds(4 * cb + j, NDP, stride=16), :] = grad_slots[
                NDP * j : NDP * j + NDP, 128 * cb : 128 * cb + 128
            ]
    gt_send[...] = rows_f[...].astype(BF).reshape(NDP, 16, 128)

    def send_grad(k, carry):
        p = lax.rem(dp + k, NDP)
        send(gt_send.at[p], gt_recv.at[dp], send_sem.at[6], recv_sem.at[4], (p, rep))
        return carry

    lax.fori_loop(1, NDP, send_grad, 0)
    gt_recv[dp] = gt_send[dp]

    mine = []
    for part in range(3):
        drain(sib_recv.at[part], sib_sem.at[part])
        for k in range(NX):
            xx = lax.rem(x + 1 + k, NX)
            total = g_all[core, part, xx].astype(F32) + sib_recv[part, xx].astype(F32)
            if k < NX - 1:
                g_all[core, part, xx] = total.astype(BF)
                send(
                    g_all.at[core, part, xx],
                    x_recv.at[part, k],
                    send_sem.at[5],
                    x_sem.at[part],
                    (dp_of(z, xx, yh), rep),
                )
        mine.append(total)

    layer_out[...] = (tokens + dot(context, wo[...], 1, 1)).astype(BF)
    outputs = (
        (layer_out, layer_out_h),
        (gt_recv, pooled_grad_h),
        (grad_qkv, grad_qkv_h),
        (grad_out, grad_out_h),
    )

    def store(i):
        return pltpu.make_async_copy(*outputs[i], out_sem.at[i])

    store(0).start()

    for part in range(3):
        drain(x_recv.at[part], x_sem.at[part])
        total = mine[part]
        for k in range(NX - 1):
            total = total + x_recv[part, k].astype(F32)
        s2[part] = total.astype(BF).reshape(NZ, 2, 16, 128)
        for k in range(1, NZ):
            zz = lax.rem(z + k, NZ)
            send(
                s2.at[part, zz],
                z_recv.at[part, k - 1],
                send_sem.at[7],
                z_sem.at[part],
                (dp_of(zz, x, yh), rep),
            )

    for part in range(3):
        total = s2[part, z].astype(F32)
        drain(z_recv.at[part], z_sem.at[part])
        for k in range(NZ - 1):
            total = total + z_recv[part, k].astype(F32)
        s3[part] = total.astype(BF)
        for k in range(1, NY):
            hh, who = y_peer(k)
            send(s3.at[part, hh], y_recv.at[part, k - 1], send_sem.at[8], y_sem.at[part], who)
    drain(gt_recv.at[pl.ds(0, NDP - 1)], recv_sem.at[4])
    store(1).start()
    for part in range(3):
        total = s3[part, yh].astype(F32)
        drain(y_recv.at[part], y_sem.at[part])
        for k in range(NY - 1):
            total = total + y_recv[part, k].astype(F32)
        fin[core, part] = total * (1.0 / SAMPLES)
    send(fin.at[core], fin.at[core], send_sem.at[9], fin_sem.at[0], sib)

    drain(fin.at[other], fin_sem.at[0])
    for cb in range(12):
        piece = fin[cb // 6, (cb % 6) // 2, 8 * (cb % 2) : 8 * (cb % 2) + 8, :]
        if cb < 9:
            grad_qkv[:, 128 * cb : 128 * cb + 128] = piece
        else:
            grad_out[:, 128 * (cb - 9) : 128 * (cb - 9) + 128] = piece
    store(2).start()
    store(3).start()

    drain(w_all.at[core, pl.ds(0, 3), x, pl.ds(0, 15)], send_sem.at[0])
    drain(tok_send.at[pl.ds(0, NDP - 1)], send_sem.at[1])
    drain(w_all.at[core, pl.ds(0, 3), pl.ds(0, 3)], send_sem.at[2])
    drain(w_all.at[core], send_sem.at[3])
    drain(sib_recv, send_sem.at[4])
    drain(x_recv, send_sem.at[5])
    drain(gt_send.at[pl.ds(0, NDP - 1)], send_sem.at[6])
    drain(z_recv, send_sem.at[7])
    drain(y_recv, send_sem.at[8])
    drain(fin.at[core], send_sem.at[9])
    for i in range(4):
        store(i).wait()


def finish(layer_in, pooled_in, qkv_in, out_in, layer_out, pooled_grad, grad_qkv, grad_out):
    layer_out[...] = layer_in[...]
    grad_qkv[...] = qkv_in[...]
    grad_out[...] = out_in[...]
    for cb in range(4):
        pooled_grad[:, :, 128 * cb : 128 * cb + 128] = pooled_in[:, 4 * cb : 4 * cb + 4, :]


def on_device(tables, sample_ids, table_slot, norm_gain, qkv_weight, out_weight, cotangent):
    vmem = pl.BlockSpec(memory_space=pltpu.VMEM)
    hbm = pl.BlockSpec(memory_space=pltpu.HBM)
    results = pl.pallas_call(
        fused,
        out_shape=(
            jax.ShapeDtypeStruct((F, E), BF),
            jax.ShapeDtypeStruct((NDP, 16, 128), BF),
            jax.ShapeDtypeStruct((8, 3 * HD), F32),
            jax.ShapeDtypeStruct((8, HD), F32),
        ),
        in_specs=[hbm] * 4 + [vmem] * 2 + [hbm],
        out_specs=(hbm,) * 4,
        scratch_shapes=[
            pltpu.VMEM((4, F, E), BF),
            pltpu.VMEM((16, NDP), jnp.int32),
            pltpu.VMEM((1, F), jnp.int32),
            pltpu.VMEM((1, E), F32),
            pltpu.VMEM((F, E), BF),
            pltpu.VMEM((NDP * 16, 128), F32),
            pltpu.VMEM((NDP, 16, 128), BF),
            pltpu.VMEM((NDP, 16, 128), BF),
            pltpu.VMEM((NDP, 16, 128), BF),
            pltpu.VMEM((NDP, 16, 128), BF),
            pltpu.VMEM((2, 3, 16, 128), BF),
            pltpu.VMEM((2, 3, NX, 16, 16, 128), BF),
            pltpu.VMEM((E, 3 * HD), BF),
            pltpu.VMEM((E, HD), BF),
            pltpu.VMEM((2, 3, NX, 16, 16, 128), BF),
            pltpu.VMEM((3, NX, 16, 16, 128), BF),
            pltpu.VMEM((3, NX - 1, 16, 16, 128), BF),
            pltpu.VMEM((3, NZ, 2, 16, 128), BF),
            pltpu.VMEM((3, NZ - 1, 2, 16, 128), BF),
            pltpu.VMEM((3, 2, 16, 128), BF),
            pltpu.VMEM((3, NY - 1, 16, 128), BF),
            pltpu.VMEM((2, 3, 16, 128), F32),
            pltpu.SemaphoreType.DMA((10,)),
            pltpu.SemaphoreType.DMA((5,)),
            pltpu.SemaphoreType.DMA((3,)),
            pltpu.SemaphoreType.DMA((3, 3)),
            pltpu.SemaphoreType.DMA((3,)),
            pltpu.SemaphoreType.DMA((3,)),
            pltpu.SemaphoreType.DMA((3,)),
            pltpu.SemaphoreType.DMA((3,)),
            pltpu.SemaphoreType.DMA((3,)),
            pltpu.SemaphoreType.DMA((1,)),
            pltpu.SemaphoreType.DMA((5,)),
            pltpu.VMEM((F, E), BF),
            pltpu.VMEM((8, 3 * HD), F32),
            pltpu.VMEM((8, HD), F32),
            pltpu.SemaphoreType.DMA((4,)),
        ],
        compiler_params=pltpu.CompilerParams(
            collective_id=0, has_side_effects=True, vmem_limit_bytes=56 * 1024 * 1024
        ),
        cost_estimate=pl.CostEstimate(
            flops=2_000_000_000, bytes_accessed=4_000_000, transcendentals=400_000
        ),
    )(
        tables,
        jnp.transpose(sample_ids, (1, 2, 0)).reshape(16, NDP),
        table_slot.reshape(1, F),
        norm_gain.reshape(1, E),
        qkv_weight,
        out_weight,
        cotangent.reshape(F, E),
    )
    layer_out, pooled_grad, grad_qkv, grad_out = pl.pallas_call(
        finish,
        out_shape=(
            jax.ShapeDtypeStruct((F, E), BF),
            jax.ShapeDtypeStruct((NDP, 4, E), BF),
            jax.ShapeDtypeStruct((8, 3 * HD), F32),
            jax.ShapeDtypeStruct((8, HD), F32),
        ),
        in_specs=[vmem] * 4,
        out_specs=(vmem,) * 4,
        compiler_params=pltpu.CompilerParams(vmem_limit_bytes=56 * 1024 * 1024),
    )(*results)
    return (layer_out.reshape(1, F, E), pooled_grad, grad_qkv, grad_out)


def solution(mesh):
    return jax.shard_map(
        on_device,
        mesh=mesh,
        in_specs=(
            P("dp", None, None),
            P("rep", "dp", None),
            P(),
            P(),
            P("dp", None),
            P("dp", None),
            P(("rep", "dp"), None, None),
        ),
        out_specs=(
            P(("rep", "dp"), None, None),
            P("rep", "dp", None),
            P("dp", None),
            P("dp", None),
        ),
        check_vma=False,
    )
```

```python
import jax
import jax.numpy as jnp
from jax import lax
from jax.experimental import pallas as pl
from jax.experimental.pallas import tpu as pltpu
from jax.sharding import PartitionSpec as P

E = 512
H = 6
DH = 64
F = 256
P_SIZE = 4
HD = H * DH
SAMPLES = 512
EPS = 1e-06

NX = 4
NZ = 8
NY = 8
NDP = 64

BF = jnp.bfloat16
F32 = jnp.float32
MESH = pl.DeviceIdType.MESH


def dot(a, b, ca, cb):
    return lax.dot_general(a, b, (((ca,), (cb,)), ((), ())), preferred_element_type=F32)


def fused(
    tables_h,
    ids_h,
    slot_h,
    gain_h,
    qkv,
    outw,
    cot_h,
    layer_out_h,
    pooled_grad_h,
    grad_qkv_h,
    grad_out_h,
    tables,
    ids,
    slot,
    gain,
    cot,
    rows_f,
    tok_send,
    tok_recv,
    gt_send,
    gt_recv,
    w_send,
    w_all,
    wp,
    g_all,
    sib_recv,
    x_recv,
    s2,
    z_recv,
    s3,
    y_recv,
    fin,
    send_sem,
    recv_sem,
    w_sem,
    wx_sem,
    ws_sem,
    sib_sem,
    x_sem,
    z_sem,
    y_sem,
    fin_sem,
    in_sem,
    layer_out,
    grad_qkv,
    grad_out,
    out_sem,
):
    dp = lax.axis_index("dp")
    rep = lax.axis_index("rep")
    z = dp // 8
    x = lax.rem(dp // 2, 4)
    yh = lax.rem(dp, 2)
    yl = rep // 2
    core = lax.rem(rep, 2)
    other = 1 - core
    y = yh * 4 + yl
    sib = (dp, yl * 2 + other)

    def dp_of(zz, xx, hh):
        return zz * 8 + xx * 2 + hh

    def y_peer(k):
        yy = lax.rem(y + k, NY)
        return yy // 4, (dp_of(z, x, yy // 4), lax.rem(yy, 4) * 2 + core)

    def send(src, dst, ssem, rsem, who):
        pltpu.make_async_remote_copy(
            src_ref=src,
            dst_ref=dst,
            send_sem=ssem,
            recv_sem=rsem,
            device_id=who,
            device_id_type=MESH,
        ).start()

    def drain(ref, sem):
        pltpu.make_async_copy(ref, ref, sem).wait()

    barrier = pltpu.get_barrier_semaphore()

    def greet(k, carry):
        pl.semaphore_signal(
            barrier, inc=1, device_id=(lax.rem(dp + k, NDP), rep), device_id_type=MESH
        )
        return carry

    lax.fori_loop(1, NDP, greet, 0)
    pl.semaphore_signal(barrier, inc=1, device_id=sib, device_id_type=MESH)
    for k in range(1, NY):
        pl.semaphore_signal(barrier, inc=1, device_id=y_peer(k)[1], device_id_type=MESH)

    def load(i, src, dst):
        pltpu.make_async_copy(src, dst, in_sem.at[i]).start()

    def loaded(i, src, dst):
        pltpu.make_async_copy(src, dst, in_sem.at[i]).wait()

    inputs = (
        (ids_h, ids),
        (tables_h, tables),
        (slot_h, slot),
        (gain_h, gain),
        (cot_h, cot),
    )
    for i, (src, dst) in enumerate(inputs):
        load(i, src, dst)

    wide = jnp.concatenate([qkv[...].astype(F32), outw[...].astype(F32)], axis=1)
    for part in range(3):
        for c in range(2):
            first, second = 128 * (6 * c + part), 128 * (6 * c + part + 3)
            w_send[c, part] = jnp.concatenate(
                [wide[:, first : first + 128], wide[:, second : second + 128]], axis=0
            ).astype(BF)
    for part in range(3):
        w_all[core, part, x, z * 2 + yh] = w_send[core, part]

    pl.semaphore_wait(barrier, NDP - 1 + 1 + NY - 1)

    for part in range(3):
        for k in range(1, 16):
            q = lax.rem(z * 2 + yh + k, 16)
            send(
                w_send.at[core, part],
                w_all.at[core, part, x, z * 2 + yh],
                send_sem.at[0],
                w_sem.at[part],
                (dp_of(q // 2, x, lax.rem(q, 2)), rep),
            )

    loaded(0, *inputs[0])
    loaded(1, *inputs[1])
    row_iota = lax.broadcasted_iota(jnp.int32, (F, NDP), 0)
    for j in range(4):
        counts = jnp.zeros((F, NDP), F32)
        for p in range(P_SIZE):
            counts = counts + jnp.where(row_iota == ids[4 * j + p : 4 * j + p + 1, :], 1.0, 0.0)
        pooled = dot(counts.astype(BF), tables[j], 0, 0) * 0.5
        for cb in range(4):
            rows_f[pl.ds(4 * j + cb, NDP, stride=16), :] = pooled[:, 128 * cb : 128 * cb + 128]
    tok_send[...] = rows_f[...].astype(BF).reshape(NDP, 16, 128)
    tok_recv[dp] = tok_send[dp]

    def send_tok(k, carry):
        p = lax.rem(dp + k, NDP)
        send(tok_send.at[p], tok_recv.at[dp], send_sem.at[1], recv_sem.at[1], (p, rep))
        return carry

    lax.fori_loop(1, NDP, send_tok, 0)

    def to_sibling(part, xx):
        block = w_all.at[core, part, xx]
        send(block, block, send_sem.at[3], ws_sem.at[part], sib)

    def forward(part):
        for k in (1, 3, 2):
            xx = lax.rem(x + NX - k, NX)
            drain(w_all.at[core, part, xx], wx_sem.at[part, k - 1])
            to_sibling(part, xx)

    for part in range(3):
        block = w_all.at[core, part, x]
        drain(w_all.at[core, part, x, pl.ds(0, 15)], w_sem.at[part])
        for k in (1, 3, 2):
            send(
                block,
                block,
                send_sem.at[2],
                wx_sem.at[part, k - 1],
                (dp_of(z, lax.rem(x + k, NX), yh), rep),
            )
        to_sibling(part, x)
    forward(0)
    loaded(2, *inputs[2])
    loaded(3, *inputs[3])
    loaded(4, *inputs[4])
    slot_iota = lax.broadcasted_iota(jnp.int32, (F, F), 0)
    place = jnp.where(slot_iota == slot[...], 1.0, 0.0).astype(BF)
    cot_t = cot[...].T

    drain(tok_recv.at[pl.ds(0, NDP - 1)], recv_sem.at[1])
    rows_f[...] = tok_recv[...].reshape(NDP * 16, 128).astype(F32)
    by_slot = jnp.concatenate(
        [rows_f[pl.ds(cb, F, stride=4), :] for cb in range(4)], axis=1
    ).astype(BF)
    tokens = dot(place, by_slot, 0, 0)
    inv = lax.rsqrt(jnp.mean(tokens * tokens, axis=-1, keepdims=True) + EPS)
    normed = tokens * inv
    gains = gain[...]
    hidden = (normed * gains).astype(BF)

    hidden_t = hidden.T

    def whole(part):
        drain(w_all.at[other, part], ws_sem.at[part])
        for c in range(2):
            for xx in range(NX):
                both = w_all[c, part, xx].astype(F32).reshape(NZ, 2, 2, 8, 128)
                for half in range(2):
                    block = both[:, :, half].reshape(NZ, 16, 128).astype(BF)
                    c0 = 256 * c + 128 * half
                    for zz in range(NZ):
                        r0 = 64 * zz + 16 * xx
                        wp[part, r0 : r0 + 16, c0 : c0 + 128] = block[zz]

    low = lax.broadcasted_iota(jnp.int32, (F, 128), 1) < DH
    zero = jnp.zeros((F, 128), BF)

    def attend(part):
        projected = dot(hidden, wp[part, :, : 3 * 128], 1, 0).astype(BF)
        q2, k2, v2 = projected[:, :128], projected[:, 128:256], projected[:, 256:]
        c2 = dot(cot[...], wp[part, :, 3 * 128 :], 1, 0).astype(BF)
        parts = []
        for half in range(2):
            mine = low if half == 0 else jnp.logical_not(low)
            scores = dot(jnp.where(mine, q2, zero), k2, 1, 1) * DH ** (-0.5)
            raised = jnp.exp(scores - jnp.max(scores, axis=-1, keepdims=True))
            soft = (raised / jnp.sum(raised, axis=-1, keepdims=True)).astype(BF)
            context = dot(soft, v2, 1, 0)
            grad_soft = dot(jnp.where(mine, c2, zero), v2, 1, 1)
            soft_f = soft.astype(F32)
            inner = jnp.sum(soft_f * grad_soft, axis=-1, keepdims=True)
            gs = (soft_f * (grad_soft - inner) * DH ** (-0.5)).astype(BF)
            parts.append((context, dot(gs, k2, 1, 0), dot(gs, q2, 0, 0), dot(soft, c2, 0, 0)))
        context, gq, gk, gv = (jnp.where(low, u, v).astype(BF) for u, v in zip(*parts))
        return context, jnp.concatenate([gq, gk, gv], axis=1)

    def terms(part, context, grad_projected):
        heads = dot(hidden_t, grad_projected, 1, 0)
        blocks = (
            heads[:, :128],
            heads[:, 128:256],
            heads[:, 256:],
            dot(cot_t, context, 1, 0),
        )
        blocks = [g.reshape(NZ, NX, 2, 8, 128) for g in blocks]
        for c in range(2):
            both = jnp.concatenate(blocks[2 * c : 2 * c + 2], axis=3).astype(BF)
            for xx in range(NX):
                g_all[c, part, xx] = both[:, xx].reshape(16, 16, 128)
        send(g_all.at[other, part], sib_recv.at[part], send_sem.at[4], sib_sem.at[part], sib)

    def over_x(part):
        drain(sib_recv.at[part], sib_sem.at[part])
        for k in range(NX):
            xx = lax.rem(x + 1 + k, NX)
            total = g_all[core, part, xx].astype(F32) + sib_recv[part, xx].astype(F32)
            if k < NX - 1:
                g_all[core, part, xx] = total.astype(BF)
                send(
                    g_all.at[core, part, xx],
                    x_recv.at[part, k],
                    send_sem.at[5],
                    x_sem.at[part],
                    (dp_of(z, xx, yh), rep),
                )
        return total

    forward(1)
    whole(0)
    context0, gp0 = attend(0)
    terms(0, context0, gp0)
    forward(2)
    whole(1)
    context1, gp1 = attend(1)
    terms(1, context1, gp1)
    mine = [over_x(0)]
    whole(2)
    context2, gp2 = attend(2)
    terms(2, context2, gp2)
    mine.append(over_x(1))

    grad_hidden = dot(gp0, wp[0, :, : 3 * 128], 1, 1)
    grad_hidden = grad_hidden + dot(gp1, wp[1, :, : 3 * 128], 1, 1)
    grad_hidden = grad_hidden + dot(gp2, wp[2, :, : 3 * 128], 1, 1)
    scaled = grad_hidden * gains
    grad_norm = inv * (scaled - normed * jnp.mean(scaled * normed, axis=-1, keepdims=True))
    grad_tokens = (cot[...].astype(F32) + grad_norm).astype(BF)
    turned = lax.rem(slot_iota, NDP) * 4 + slot_iota // NDP
    place_back = jnp.where(turned == slot[...], 1.0, 0.0).astype(BF)
    grad_slots = dot(place_back, grad_tokens, 1, 0)
    for cb in range(4):
        for j in range(4):
            rows_f[pl.ds(4 * cb + j, NDP, stride=16), :] = grad_slots[
                NDP * j : NDP * j + NDP, 128 * cb : 128 * cb + 128
            ]
    gt_send[...] = rows_f[...].astype(BF).reshape(NDP, 16, 128)

    def send_grad(k, carry):
        p = lax.rem(dp + k, NDP)
        send(gt_send.at[p], gt_recv.at[dp], send_sem.at[6], recv_sem.at[4], (p, rep))
        return carry

    lax.fori_loop(1, NDP, send_grad, 0)
    gt_recv[dp] = gt_send[dp]

    mine.append(over_x(2))

    branch = dot(context0, wp[0, :, 3 * 128 :], 1, 1)
    branch = branch + dot(context1, wp[1, :, 3 * 128 :], 1, 1)
    branch = branch + dot(context2, wp[2, :, 3 * 128 :], 1, 1)
    layer_out[...] = (tokens + branch).astype(BF)
    outputs = (
        (layer_out, layer_out_h),
        (gt_recv, pooled_grad_h),
        (grad_qkv, grad_qkv_h),
        (grad_out, grad_out_h),
    )

    def store(i):
        return pltpu.make_async_copy(*outputs[i], out_sem.at[i])

    store(0).start()

    for part in range(3):
        drain(x_recv.at[part], x_sem.at[part])
        total = mine[part]
        for k in range(NX - 1):
            total = total + x_recv[part, k].astype(F32)
        s2[part] = total.astype(BF).reshape(NZ, 2, 16, 128)
        for k in range(1, NZ):
            zz = lax.rem(z + k, NZ)
            send(
                s2.at[part, zz],
                z_recv.at[part, k - 1],
                send_sem.at[7],
                z_sem.at[part],
                (dp_of(zz, x, yh), rep),
            )

    for part in range(3):
        total = s2[part, z].astype(F32)
        drain(z_recv.at[part], z_sem.at[part])
        for k in range(NZ - 1):
            total = total + z_recv[part, k].astype(F32)
        s3[part] = total.astype(BF)
        for k in range(1, NY):
            hh, who = y_peer(k)
            send(s3.at[part, hh], y_recv.at[part, k - 1], send_sem.at[8], y_sem.at[part], who)
    drain(gt_recv.at[pl.ds(0, NDP - 1)], recv_sem.at[4])
    store(1).start()
    for part in range(3):
        total = s3[part, yh].astype(F32)
        drain(y_recv.at[part], y_sem.at[part])
        for k in range(NY - 1):
            total = total + y_recv[part, k].astype(F32)
        fin[core, part] = total * (1.0 / SAMPLES)
    send(fin.at[core], fin.at[core], send_sem.at[9], fin_sem.at[0], sib)

    drain(fin.at[other], fin_sem.at[0])
    for cb in range(12):
        half = 8 * (cb % 6 // 3)
        piece = fin[cb // 6, cb % 3, half : half + 8, :]
        if cb < 9:
            grad_qkv[:, 128 * cb : 128 * cb + 128] = piece
        else:
            grad_out[:, 128 * (cb - 9) : 128 * (cb - 9) + 128] = piece
    store(2).start()
    store(3).start()

    drain(w_all.at[core, pl.ds(0, 3), x, pl.ds(0, 15)], send_sem.at[0])
    drain(tok_send.at[pl.ds(0, NDP - 1)], send_sem.at[1])
    drain(w_all.at[core, pl.ds(0, 3), pl.ds(0, 3)], send_sem.at[2])
    drain(w_all.at[core], send_sem.at[3])
    drain(sib_recv, send_sem.at[4])
    drain(x_recv, send_sem.at[5])
    drain(gt_send.at[pl.ds(0, NDP - 1)], send_sem.at[6])
    drain(z_recv, send_sem.at[7])
    drain(y_recv, send_sem.at[8])
    drain(fin.at[core], send_sem.at[9])
    for i in range(4):
        store(i).wait()


def finish(layer_in, pooled_in, qkv_in, out_in, layer_out, pooled_grad, grad_qkv, grad_out):
    layer_out[...] = layer_in[...]
    grad_qkv[...] = qkv_in[...]
    grad_out[...] = out_in[...]
    for cb in range(4):
        pooled_grad[:, :, 128 * cb : 128 * cb + 128] = pooled_in[:, 4 * cb : 4 * cb + 4, :]


def on_device(tables, sample_ids, table_slot, norm_gain, qkv_weight, out_weight, cotangent):
    vmem = pl.BlockSpec(memory_space=pltpu.VMEM)
    hbm = pl.BlockSpec(memory_space=pltpu.HBM)
    results = pl.pallas_call(
        fused,
        out_shape=(
            jax.ShapeDtypeStruct((F, E), BF),
            jax.ShapeDtypeStruct((NDP, 16, 128), BF),
            jax.ShapeDtypeStruct((8, 3 * HD), F32),
            jax.ShapeDtypeStruct((8, HD), F32),
        ),
        in_specs=[hbm] * 4 + [vmem] * 2 + [hbm],
        out_specs=(hbm,) * 4,
        scratch_shapes=[
            pltpu.VMEM((4, F, E), BF),
            pltpu.VMEM((16, NDP), jnp.int32),
            pltpu.VMEM((1, F), jnp.int32),
            pltpu.VMEM((1, E), F32),
            pltpu.VMEM((F, E), BF),
            pltpu.VMEM((NDP * 16, 128), F32),
            pltpu.VMEM((NDP, 16, 128), BF),
            pltpu.VMEM((NDP, 16, 128), BF),
            pltpu.VMEM((NDP, 16, 128), BF),
            pltpu.VMEM((NDP, 16, 128), BF),
            pltpu.VMEM((2, 3, 16, 128), BF),
            pltpu.VMEM((2, 3, NX, 16, 16, 128), BF),
            pltpu.VMEM((3, E, 4 * 128), BF),
            pltpu.VMEM((2, 3, NX, 16, 16, 128), BF),
            pltpu.VMEM((3, NX, 16, 16, 128), BF),
            pltpu.VMEM((3, NX - 1, 16, 16, 128), BF),
            pltpu.VMEM((3, NZ, 2, 16, 128), BF),
            pltpu.VMEM((3, NZ - 1, 2, 16, 128), BF),
            pltpu.VMEM((3, 2, 16, 128), BF),
            pltpu.VMEM((3, NY - 1, 16, 128), BF),
            pltpu.VMEM((2, 3, 16, 128), F32),
            pltpu.SemaphoreType.DMA((10,)),
            pltpu.SemaphoreType.DMA((5,)),
            pltpu.SemaphoreType.DMA((3,)),
            pltpu.SemaphoreType.DMA((3, 3)),
            pltpu.SemaphoreType.DMA((3,)),
            pltpu.SemaphoreType.DMA((3,)),
            pltpu.SemaphoreType.DMA((3,)),
            pltpu.SemaphoreType.DMA((3,)),
            pltpu.SemaphoreType.DMA((3,)),
            pltpu.SemaphoreType.DMA((1,)),
            pltpu.SemaphoreType.DMA((5,)),
            pltpu.VMEM((F, E), BF),
            pltpu.VMEM((8, 3 * HD), F32),
            pltpu.VMEM((8, HD), F32),
            pltpu.SemaphoreType.DMA((4,)),
        ],
        compiler_params=pltpu.CompilerParams(
            collective_id=0, has_side_effects=True, vmem_limit_bytes=56 * 1024 * 1024
        ),
        cost_estimate=pl.CostEstimate(
            flops=2_000_000_000, bytes_accessed=4_000_000, transcendentals=400_000
        ),
    )(
        tables,
        jnp.transpose(sample_ids, (1, 2, 0)).reshape(16, NDP),
        table_slot.reshape(1, F),
        norm_gain.reshape(1, E),
        qkv_weight,
        out_weight,
        cotangent.reshape(F, E),
    )
    layer_out, pooled_grad, grad_qkv, grad_out = pl.pallas_call(
        finish,
        out_shape=(
            jax.ShapeDtypeStruct((F, E), BF),
            jax.ShapeDtypeStruct((NDP, 4, E), BF),
            jax.ShapeDtypeStruct((8, 3 * HD), F32),
            jax.ShapeDtypeStruct((8, HD), F32),
        ),
        in_specs=[vmem] * 4,
        out_specs=(vmem,) * 4,
        compiler_params=pltpu.CompilerParams(vmem_limit_bytes=56 * 1024 * 1024),
    )(*results)
    return (layer_out.reshape(1, F, E), pooled_grad, grad_qkv, grad_out)


def solution(mesh):
    return jax.shard_map(
        on_device,
        mesh=mesh,
        in_specs=(
            P("dp", None, None),
            P("rep", "dp", None),
            P(),
            P(),
            P("dp", None),
            P("dp", None),
            P(("rep", "dp"), None, None),
        ),
        out_specs=(
            P(("rep", "dp"), None, None),
            P("rep", "dp", None),
            P("dp", None),
            P("dp", None),
        ),
        check_vma=False,
    )
```

```python
import jax
import jax.numpy as jnp
from jax import lax
from jax.experimental import pallas as pl
from jax.experimental.pallas import tpu as pltpu
from jax.sharding import PartitionSpec as P

E = 512
H = 6
DH = 64
F = 256
P_SIZE = 4
HD = H * DH
SAMPLES = 512
EPS = 1e-06

NX = 4
NZ = 8
NY = 8
NDP = 64

BF = jnp.bfloat16
F32 = jnp.float32
MESH = pl.DeviceIdType.MESH


def dot(a, b, ca, cb):
    return lax.dot_general(a, b, (((ca,), (cb,)), ((), ())), preferred_element_type=F32)


def fused(
    tables_h,
    ids_h,
    slot_h,
    gain_h,
    qkv,
    outw,
    cot_h,
    layer_out_h,
    pooled_grad_h,
    grad_qkv_h,
    grad_out_h,
    tables,
    ids,
    slot,
    gain,
    cot,
    rows_f,
    tok_send,
    tok_recv,
    gt_send,
    gt_recv,
    w_send,
    w_all,
    wp,
    g_all,
    sib_recv,
    x_recv,
    s2,
    z_recv,
    s3,
    y_recv,
    fin,
    send_sem,
    recv_sem,
    w_sem,
    wx_sem,
    ws_sem,
    sib_sem,
    x_sem,
    z_sem,
    y_sem,
    fin_sem,
    in_sem,
    layer_out,
    grad_qkv,
    grad_out,
    out_sem,
):
    dp = lax.axis_index("dp")
    rep = lax.axis_index("rep")
    z = dp // 8
    x = lax.rem(dp // 2, 4)
    yh = lax.rem(dp, 2)
    yl = rep // 2
    core = lax.rem(rep, 2)
    other = 1 - core
    y = yh * 4 + yl
    sib = (dp, yl * 2 + other)

    def dp_of(zz, xx, hh):
        return zz * 8 + xx * 2 + hh

    def y_peer(k):
        yy = lax.rem(y + k, NY)
        return yy // 4, (dp_of(z, x, yy // 4), lax.rem(yy, 4) * 2 + core)

    def send(src, dst, ssem, rsem, who):
        pltpu.make_async_remote_copy(
            src_ref=src,
            dst_ref=dst,
            send_sem=ssem,
            recv_sem=rsem,
            device_id=who,
            device_id_type=MESH,
        ).start()

    def drain(ref, sem):
        pltpu.make_async_copy(ref, ref, sem).wait()

    barrier = pltpu.get_barrier_semaphore()

    def greet(k, carry):
        pl.semaphore_signal(
            barrier, inc=1, device_id=(lax.rem(dp + k, NDP), rep), device_id_type=MESH
        )
        return carry

    lax.fori_loop(1, NDP, greet, 0)
    pl.semaphore_signal(barrier, inc=1, device_id=sib, device_id_type=MESH)
    for k in range(1, NY):
        pl.semaphore_signal(barrier, inc=1, device_id=y_peer(k)[1], device_id_type=MESH)

    def load(i, src, dst):
        pltpu.make_async_copy(src, dst, in_sem.at[i]).start()

    def loaded(i, src, dst):
        pltpu.make_async_copy(src, dst, in_sem.at[i]).wait()

    inputs = (
        (ids_h, ids),
        (tables_h, tables),
        (slot_h, slot),
        (gain_h, gain),
        (cot_h, cot),
    )
    for i, (src, dst) in enumerate(inputs):
        load(i, src, dst)

    wide = jnp.concatenate([qkv[...].astype(F32), outw[...].astype(F32)], axis=1)
    for part in range(3):
        for c in range(2):
            first, second = 128 * (6 * c + part), 128 * (6 * c + part + 3)
            w_send[c, part] = jnp.concatenate(
                [wide[:, first : first + 128], wide[:, second : second + 128]], axis=0
            ).astype(BF)
    for part in range(3):
        w_all[core, part, x, z * 2 + yh] = w_send[core, part]

    pl.semaphore_wait(barrier, NDP - 1 + 1 + NY - 1)

    for part in range(3):
        for k in range(1, 16):
            q = lax.rem(z * 2 + yh + k, 16)
            send(
                w_send.at[core, part],
                w_all.at[core, part, x, z * 2 + yh],
                send_sem.at[0],
                w_sem.at[part],
                (dp_of(q // 2, x, lax.rem(q, 2)), rep),
            )

    loaded(0, *inputs[0])
    loaded(1, *inputs[1])
    row_iota = lax.broadcasted_iota(jnp.int32, (F, NDP), 0)
    for j in range(4):
        counts = jnp.zeros((F, NDP), F32)
        for p in range(P_SIZE):
            counts = counts + jnp.where(row_iota == ids[4 * j + p : 4 * j + p + 1, :], 1.0, 0.0)
        pooled = dot(counts.astype(BF), tables[j], 0, 0) * 0.5
        for cb in range(4):
            rows_f[pl.ds(4 * j + cb, NDP, stride=16), :] = pooled[:, 128 * cb : 128 * cb + 128]
    tok_send[...] = rows_f[...].astype(BF).reshape(NDP, 16, 128)
    tok_recv[dp] = tok_send[dp]

    def send_tok(k, carry):
        p = lax.rem(dp + k, NDP)
        send(tok_send.at[p], tok_recv.at[dp], send_sem.at[1], recv_sem.at[1], (p, rep))
        return carry

    lax.fori_loop(1, NDP, send_tok, 0)

    def to_sibling(part, xx):
        block = w_all.at[core, part, xx]
        send(block, block, send_sem.at[3], ws_sem.at[part], sib)

    def forward(part):
        for k in (1, 3, 2):
            xx = lax.rem(x + NX - k, NX)
            drain(w_all.at[core, part, xx], wx_sem.at[part, k - 1])
            to_sibling(part, xx)

    for part in range(3):
        block = w_all.at[core, part, x]
        drain(w_all.at[core, part, x, pl.ds(0, 15)], w_sem.at[part])
        for k in (1, 3, 2):
            send(
                block,
                block,
                send_sem.at[2],
                wx_sem.at[part, k - 1],
                (dp_of(z, lax.rem(x + k, NX), yh), rep),
            )
        to_sibling(part, x)
    forward(0)
    loaded(2, *inputs[2])
    loaded(3, *inputs[3])
    loaded(4, *inputs[4])
    slot_iota = lax.broadcasted_iota(jnp.int32, (F, F), 0)
    place = jnp.where(slot_iota == slot[...], 1.0, 0.0).astype(BF)
    cot_t = cot[...].T

    drain(tok_recv.at[pl.ds(0, NDP - 1)], recv_sem.at[1])
    rows_f[...] = tok_recv[...].reshape(NDP * 16, 128).astype(F32)
    by_slot = jnp.concatenate(
        [rows_f[pl.ds(cb, F, stride=4), :] for cb in range(4)], axis=1
    ).astype(BF)
    tokens = dot(place, by_slot, 0, 0)
    inv = lax.rsqrt(jnp.mean(tokens * tokens, axis=-1, keepdims=True) + EPS)
    normed = tokens * inv
    gains = gain[...]
    hidden = (normed * gains).astype(BF)

    hidden_t = hidden.T

    def whole(part):
        drain(w_all.at[other, part], ws_sem.at[part])
        for c in range(2):
            for xx in range(NX):
                both = w_all[c, part, xx].astype(F32).reshape(NZ, 2, 2, 8, 128)
                for half in range(2):
                    block = both[:, :, half].reshape(NZ, 16, 128).astype(BF)
                    c0 = 256 * c + 128 * half
                    for zz in range(NZ):
                        r0 = 64 * zz + 16 * xx
                        wp[part, r0 : r0 + 16, c0 : c0 + 128] = block[zz]

    low = lax.broadcasted_iota(jnp.int32, (F, 128), 1) < DH
    zero = jnp.zeros((F, 128), BF)

    def attend(part):
        projected = dot(hidden, wp[part, :, : 3 * 128], 1, 0).astype(BF)
        q2, k2, v2 = projected[:, :128], projected[:, 128:256], projected[:, 256:]
        c2 = dot(cot[...], wp[part, :, 3 * 128 :], 1, 0).astype(BF)
        parts = []
        for half in range(2):
            mine = low if half == 0 else jnp.logical_not(low)
            scores = dot(jnp.where(mine, q2, zero), k2, 1, 1) * DH ** (-0.5)
            raised = jnp.exp(scores - jnp.max(scores, axis=-1, keepdims=True))
            soft = (raised / jnp.sum(raised, axis=-1, keepdims=True)).astype(BF)
            context = dot(soft, v2, 1, 0)
            grad_soft = dot(jnp.where(mine, c2, zero), v2, 1, 1)
            soft_f = soft.astype(F32)
            inner = jnp.sum(soft_f * grad_soft, axis=-1, keepdims=True)
            gs = (soft_f * (grad_soft - inner) * DH ** (-0.5)).astype(BF)
            parts.append((context, dot(gs, k2, 1, 0), dot(gs, q2, 0, 0), dot(soft, c2, 0, 0)))
        context, gq, gk, gv = (jnp.where(low, u, v).astype(BF) for u, v in zip(*parts))
        return context, jnp.concatenate([gq, gk, gv], axis=1)

    def terms(part, context, grad_projected):
        heads = dot(hidden_t, grad_projected, 1, 0)
        blocks = (
            heads[:, :128],
            heads[:, 128:256],
            heads[:, 256:],
            dot(cot_t, context, 1, 0),
        )
        blocks = [g.reshape(NZ, NX, 2, 8, 128) for g in blocks]
        for c in range(2):
            both = jnp.concatenate(blocks[2 * c : 2 * c + 2], axis=3).astype(BF)
            for xx in range(NX):
                g_all[c, part, xx] = both[:, xx].reshape(16, 16, 128)
        send(g_all.at[other, part], sib_recv.at[part], send_sem.at[4], sib_sem.at[part], sib)

    def over_x(part):
        drain(sib_recv.at[part], sib_sem.at[part])
        for k in range(NX):
            xx = lax.rem(x + 1 + k, NX)
            total = g_all[core, part, xx].astype(F32) + sib_recv[part, xx].astype(F32)
            if k < NX - 1:
                g_all[core, part, xx] = total.astype(BF)
                send(
                    g_all.at[core, part, xx],
                    x_recv.at[part, k],
                    send_sem.at[5],
                    x_sem.at[part],
                    (dp_of(z, xx, yh), rep),
                )
        return total

    forward(1)
    whole(0)
    context0, gp0 = attend(0)
    terms(0, context0, gp0)
    forward(2)
    whole(1)
    context1, gp1 = attend(1)
    terms(1, context1, gp1)
    mine = [over_x(0)]
    whole(2)
    context2, gp2 = attend(2)
    terms(2, context2, gp2)
    mine.append(over_x(1))

    def over_z(part):
        drain(x_recv.at[part], x_sem.at[part])
        total = mine[part]
        for k in range(NX - 1):
            total = total + x_recv[part, k].astype(F32)
        s2[part] = total.astype(BF).reshape(NZ, 2, 16, 128)
        for k in range(1, NZ):
            zz = lax.rem(z + k, NZ)
            send(
                s2.at[part, zz],
                z_recv.at[part, k - 1],
                send_sem.at[7],
                z_sem.at[part],
                (dp_of(zz, x, yh), rep),
            )

    grad_hidden = dot(gp0, wp[0, :, : 3 * 128], 1, 1)
    grad_hidden = grad_hidden + dot(gp1, wp[1, :, : 3 * 128], 1, 1)
    grad_hidden = grad_hidden + dot(gp2, wp[2, :, : 3 * 128], 1, 1)
    scaled = grad_hidden * gains
    grad_norm = inv * (scaled - normed * jnp.mean(scaled * normed, axis=-1, keepdims=True))
    grad_tokens = (cot[...].astype(F32) + grad_norm).astype(BF)
    turned = lax.rem(slot_iota, NDP) * 4 + slot_iota // NDP
    place_back = jnp.where(turned == slot[...], 1.0, 0.0).astype(BF)
    grad_slots = dot(place_back, grad_tokens, 1, 0)
    for cb in range(4):
        for j in range(4):
            rows_f[pl.ds(4 * cb + j, NDP, stride=16), :] = grad_slots[
                NDP * j : NDP * j + NDP, 128 * cb : 128 * cb + 128
            ]
    gt_send[...] = rows_f[...].astype(BF).reshape(NDP, 16, 128)

    mine.append(over_x(2))
    over_z(0)

    def send_grad(k, carry):
        p = lax.rem(dp + k, NDP)
        send(gt_send.at[p], gt_recv.at[dp], send_sem.at[6], recv_sem.at[4], (p, rep))
        return carry

    lax.fori_loop(1, NDP, send_grad, 0)
    gt_recv[dp] = gt_send[dp]

    over_z(1)
    branch = dot(context0, wp[0, :, 3 * 128 :], 1, 1)
    branch = branch + dot(context1, wp[1, :, 3 * 128 :], 1, 1)
    branch = branch + dot(context2, wp[2, :, 3 * 128 :], 1, 1)
    layer_out[...] = (tokens + branch).astype(BF)
    outputs = (
        (layer_out, layer_out_h),
        (gt_recv, pooled_grad_h),
        (grad_qkv, grad_qkv_h),
        (grad_out, grad_out_h),
    )

    def store(i):
        return pltpu.make_async_copy(*outputs[i], out_sem.at[i])

    store(0).start()
    over_z(2)

    for part in range(3):
        total = s2[part, z].astype(F32)
        drain(z_recv.at[part], z_sem.at[part])
        for k in range(NZ - 1):
            total = total + z_recv[part, k].astype(F32)
        s3[part] = total.astype(BF)
        for k in range(1, NY):
            hh, who = y_peer(k)
            send(s3.at[part, hh], y_recv.at[part, k - 1], send_sem.at[8], y_sem.at[part], who)
    drain(gt_recv.at[pl.ds(0, NDP - 1)], recv_sem.at[4])
    store(1).start()
    for part in range(3):
        total = s3[part, yh].astype(F32)
        drain(y_recv.at[part], y_sem.at[part])
        for k in range(NY - 1):
            total = total + y_recv[part, k].astype(F32)
        fin[core, part] = total * (1.0 / SAMPLES)
    send(fin.at[core], fin.at[core], send_sem.at[9], fin_sem.at[0], sib)

    drain(fin.at[other], fin_sem.at[0])
    for cb in range(12):
        half = 8 * (cb % 6 // 3)
        piece = fin[cb // 6, cb % 3, half : half + 8, :]
        if cb < 9:
            grad_qkv[:, 128 * cb : 128 * cb + 128] = piece
        else:
            grad_out[:, 128 * (cb - 9) : 128 * (cb - 9) + 128] = piece
    store(2).start()
    store(3).start()

    drain(w_all.at[core, pl.ds(0, 3), x, pl.ds(0, 15)], send_sem.at[0])
    drain(tok_send.at[pl.ds(0, NDP - 1)], send_sem.at[1])
    drain(w_all.at[core, pl.ds(0, 3), pl.ds(0, 3)], send_sem.at[2])
    drain(w_all.at[core], send_sem.at[3])
    drain(sib_recv, send_sem.at[4])
    drain(x_recv, send_sem.at[5])
    drain(gt_send.at[pl.ds(0, NDP - 1)], send_sem.at[6])
    drain(z_recv, send_sem.at[7])
    drain(y_recv, send_sem.at[8])
    drain(fin.at[core], send_sem.at[9])
    for i in range(4):
        store(i).wait()


def finish(layer_in, pooled_in, qkv_in, out_in, layer_out, pooled_grad, grad_qkv, grad_out):
    layer_out[...] = layer_in[...]
    grad_qkv[...] = qkv_in[...]
    grad_out[...] = out_in[...]
    for cb in range(4):
        pooled_grad[:, :, 128 * cb : 128 * cb + 128] = pooled_in[:, 4 * cb : 4 * cb + 4, :]


def on_device(tables, sample_ids, table_slot, norm_gain, qkv_weight, out_weight, cotangent):
    vmem = pl.BlockSpec(memory_space=pltpu.VMEM)
    hbm = pl.BlockSpec(memory_space=pltpu.HBM)
    results = pl.pallas_call(
        fused,
        out_shape=(
            jax.ShapeDtypeStruct((F, E), BF),
            jax.ShapeDtypeStruct((NDP, 16, 128), BF),
            jax.ShapeDtypeStruct((8, 3 * HD), F32),
            jax.ShapeDtypeStruct((8, HD), F32),
        ),
        in_specs=[hbm] * 4 + [vmem] * 2 + [hbm],
        out_specs=(hbm,) * 4,
        scratch_shapes=[
            pltpu.VMEM((4, F, E), BF),
            pltpu.VMEM((16, NDP), jnp.int32),
            pltpu.VMEM((1, F), jnp.int32),
            pltpu.VMEM((1, E), F32),
            pltpu.VMEM((F, E), BF),
            pltpu.VMEM((NDP * 16, 128), F32),
            pltpu.VMEM((NDP, 16, 128), BF),
            pltpu.VMEM((NDP, 16, 128), BF),
            pltpu.VMEM((NDP, 16, 128), BF),
            pltpu.VMEM((NDP, 16, 128), BF),
            pltpu.VMEM((2, 3, 16, 128), BF),
            pltpu.VMEM((2, 3, NX, 16, 16, 128), BF),
            pltpu.VMEM((3, E, 4 * 128), BF),
            pltpu.VMEM((2, 3, NX, 16, 16, 128), BF),
            pltpu.VMEM((3, NX, 16, 16, 128), BF),
            pltpu.VMEM((3, NX - 1, 16, 16, 128), BF),
            pltpu.VMEM((3, NZ, 2, 16, 128), BF),
            pltpu.VMEM((3, NZ - 1, 2, 16, 128), BF),
            pltpu.VMEM((3, 2, 16, 128), BF),
            pltpu.VMEM((3, NY - 1, 16, 128), BF),
            pltpu.VMEM((2, 3, 16, 128), F32),
            pltpu.SemaphoreType.DMA((10,)),
            pltpu.SemaphoreType.DMA((5,)),
            pltpu.SemaphoreType.DMA((3,)),
            pltpu.SemaphoreType.DMA((3, 3)),
            pltpu.SemaphoreType.DMA((3,)),
            pltpu.SemaphoreType.DMA((3,)),
            pltpu.SemaphoreType.DMA((3,)),
            pltpu.SemaphoreType.DMA((3,)),
            pltpu.SemaphoreType.DMA((3,)),
            pltpu.SemaphoreType.DMA((1,)),
            pltpu.SemaphoreType.DMA((5,)),
            pltpu.VMEM((F, E), BF),
            pltpu.VMEM((8, 3 * HD), F32),
            pltpu.VMEM((8, HD), F32),
            pltpu.SemaphoreType.DMA((4,)),
        ],
        compiler_params=pltpu.CompilerParams(
            collective_id=0, has_side_effects=True, vmem_limit_bytes=56 * 1024 * 1024
        ),
        cost_estimate=pl.CostEstimate(
            flops=2_000_000_000, bytes_accessed=4_000_000, transcendentals=400_000
        ),
    )(
        tables,
        jnp.transpose(sample_ids, (1, 2, 0)).reshape(16, NDP),
        table_slot.reshape(1, F),
        norm_gain.reshape(1, E),
        qkv_weight,
        out_weight,
        cotangent.reshape(F, E),
    )
    layer_out, pooled_grad, grad_qkv, grad_out = pl.pallas_call(
        finish,
        out_shape=(
            jax.ShapeDtypeStruct((F, E), BF),
            jax.ShapeDtypeStruct((NDP, 4, E), BF),
            jax.ShapeDtypeStruct((8, 3 * HD), F32),
            jax.ShapeDtypeStruct((8, HD), F32),
        ),
        in_specs=[vmem] * 4,
        out_specs=(vmem,) * 4,
        compiler_params=pltpu.CompilerParams(vmem_limit_bytes=56 * 1024 * 1024),
    )(*results)
    return (layer_out.reshape(1, F, E), pooled_grad, grad_qkv, grad_out)


def solution(mesh):
    return jax.shard_map(
        on_device,
        mesh=mesh,
        in_specs=(
            P("dp", None, None),
            P("rep", "dp", None),
            P(),
            P(),
            P("dp", None),
            P("dp", None),
            P(("rep", "dp"), None, None),
        ),
        out_specs=(
            P(("rep", "dp"), None, None),
            P("rep", "dp", None),
            P("dp", None),
            P("dp", None),
        ),
        check_vma=False,
    )
```
